32 devices in a mesh: cfg: 2 (over y), tm: 16 (over z, x, core).
Axes of the slice: x: 2, y: 2, z: 4, core: 2. Of those that a mesh axis runs over, the one named last changes fastest.
Arguments:
- meson_fields: bfloat16 [2, 32, 32, 256, 256], P(None, None, ('cfg', 'tm')), parts along dimension 2, may hold values from -1.3 to 1.3
- perambulators: bfloat16 [2, 32, 256, 256], P(None, ('cfg', 'tm')), parts along dimension 1, may hold values from -0.25 to 0.25
- direct_ins: int32 [4096, 4], replicated, may hold values from 0 to 31, as said below
- direct_coef: float32 [4096], replicated, may hold values from -5 to 5
- direct_entry: int32 [4096], replicated, may hold values from 0 to 63
- box_ins: int32 [8, 4], replicated, may hold values from 0 to 31, as said below
- box_coef: float32 [8], replicated, may hold values from -24 to 24
- box_entry: int32 [8], replicated, may hold values from 0 to 63
Outputs:
- correlator: float32 [3, 2, 128], P(None, None, ('cfg', 'tm')), parts along dimension 2
The draws below stay inside these ranges and needn't reach their ends.
There are 2 independent parts, one for each index of `cfg`. The reference program is written for one: setup_inputs(seed, part) draws one part's arguments, and reference() takes and returns one part's arrays. A program takes and returns all parts, laid end to end along the dimension named above; an argument that names none is the same for every part. Nothing has to cross between parts.
Inputs may be any that keep to these rules, and one draw needn't show every extreme that they name: `direct_ins`: within a term, insertions 0 and 1 differ, 1 and 2 differ, 2 and 3 differ. `box_ins`: within a term, insertions 0 and 1 differ, 1 and 2 differ, 2 and 3 differ.
All inputs are finite; a program needn't handle non-finite values.
Results may differ from the reference program's by a relative error of at most 0.0046.
Values may be sent and summed in bfloat16 or wider, within the bound.
A program may use at most 192 MiB of HBM per device.

```python
import math
import jax
import jax.numpy as jnp
from jax import lax

MODES = 256
INSERTIONS = 32
SLICE_DEV = 1
SLICES = 16
SEPARATIONS = 3
DIRECT_TERMS = 4096
BOX_TERMS = 8
ENTRIES = 64


def draw_meson_fields(key, part):
    subkeys = jax.random.split(key, 3)
    field_shape = (2, INSERTIONS, SLICES, MODES, MODES)
    spread = math.sqrt(10.0)
    base_draw = jax.random.truncated_normal(subkeys[0], -6.0, 6.0, field_shape, jnp.float32)
    row_scale = jnp.exp(jax.random.uniform(subkeys[1], (1, INSERTIONS, SLICES, MODES, 1), jnp.float32, 0.0, math.log(spread)))
    col_scale = jnp.exp(jax.random.uniform(subkeys[2], (1, INSERTIONS, SLICES, 1, MODES), jnp.float32, 0.0, math.log(spread)))
    mean_square = (spread * spread - 1.0) / (2.0 * math.log(spread))
    time_ramp = jnp.arange(SLICES, dtype=jnp.float32) / max(SLICES - 1, 1)
    time_scale = jnp.exp(0.25 * math.log(3.0) * time_ramp)[None, None, :, None, None]
    values = base_draw * row_scale * col_scale * time_scale / (mean_square * math.sqrt(MODES))
    return jnp.clip(values, -1.3, 1.3).astype(jnp.bfloat16)


def draw_terms(key, term_count):
    subkeys = jax.random.split(key, 3)
    leading = jax.random.randint(subkeys[0], (term_count,), 0, INSERTIONS)
    placed = jax.random.permutation(subkeys[1], term_count)
    position = jnp.arange(term_count)
    leading = jnp.where(position == placed[0], 0, jnp.where(position == placed[1], INSERTIONS - 1, leading))
    offsets = jax.random.randint(subkeys[2], (term_count, 3), 1, INSERTIONS)
    second = (leading + offsets[:, 0]) % INSERTIONS
    third_ins = (second + offsets[:, 1]) % INSERTIONS
    fourth = (third_ins + offsets[:, 2]) % INSERTIONS
    return jnp.stack([leading, second, third_ins, fourth], axis=1).astype(jnp.int32)


def draw_direct_ins(key, part):
    return draw_terms(jax.random.fold_in(key, 17), DIRECT_TERMS)


def draw_box_ins(key, part):
    return draw_terms(jax.random.fold_in(key, 29), BOX_TERMS)


def place_ends(entries, rng, low, largest):
    longest = entries.shape.index(max(entries.shape))
    spots = []
    for shift in (0, 1):
        where = [jax.random.randint(jax.random.fold_in(rng, axis), (), 0, length) for axis, length in enumerate(entries.shape)]
        where[longest] = (where[longest] + shift) % entries.shape[longest]
        spots.append(tuple(where))
    return entries.at[spots[0]].set(low).at[spots[1]].set(largest)


def level_of(own_key, shape, cuts, smallest, largest):
    factor_of, own = 1.0, jax.random.fold_in(own_key, 6)
    for dim, parts in cuts:
        steps = jnp.exp(jax.random.uniform(jax.random.fold_in(own, dim), (parts,), jnp.float32, smallest / len(cuts), largest / len(cuts)))
        factor_of = factor_of * jnp.repeat(steps, shape[dim] // parts).reshape([-1 if axis == dim else 1 for axis in range(len(shape))])
    return factor_of


def normal_values(stream_key, dims, width, reach, shards=(), kind=jnp.bfloat16):
    gain = level_of(stream_key, dims, shards, -0.22, 0.18) if shards else 1.0
    entries = jax.random.normal(stream_key, dims, jnp.float32) * width * gain
    return jnp.minimum(jnp.maximum(entries, -reach), reach).astype(kind)


def setup_inputs(seed: int = 0, part: int = 0) -> dict:
    streams_of = jax.random.split(jax.random.key(seed), 9)
    own_keys = jax.random.split(jax.random.fold_in(streams_of[8], part), 9)
    return {
        "meson_fields": draw_meson_fields(jax.random.fold_in(jax.random.fold_in(streams_of[8], part), 71), part),
        "perambulators": normal_values(own_keys[1], (2, SLICES, MODES, MODES), (2 * MODES) ** -0.5, 0.25, ((1, 16),)),
        "direct_ins": draw_direct_ins(jax.random.fold_in(streams_of[8], 71), part),
        "direct_coef": normal_values(streams_of[3], (DIRECT_TERMS,), 1.0, 5.0, (), jnp.float32),
        "direct_entry": place_ends(jax.random.randint(streams_of[4], (DIRECT_TERMS,), 0, ENTRIES), jax.random.fold_in(streams_of[4], 1), 0, ENTRIES - 1).astype(jnp.int32),
        "box_ins": draw_box_ins(jax.random.fold_in(streams_of[8], 71), part),
        "box_coef": normal_values(streams_of[6], (BOX_TERMS,), 4.0, 24.0, (), jnp.float32),
        "box_entry": place_ends(jax.random.randint(streams_of[7], (BOX_TERMS,), 0, ENTRIES), jax.random.fold_in(streams_of[7], 1), 0, ENTRIES - 1).astype(jnp.int32),
    }


def dress(fields, propagator):
    stacked = jnp.stack([jnp.stack([propagator[0], propagator[1]], 1), jnp.stack([-propagator[1], propagator[0]], 1)], 0)
    product = jnp.einsum("cgij,cjdk->dgik", fields.astype(jnp.float32), stacked.astype(jnp.float32))
    return product.astype(jnp.bfloat16)


def adjoint_product(left_side, right_side):
    real_part = jnp.einsum("clij,clkj->lik", left_side, right_side)
    imag_part = jnp.einsum("lij,lkj->lik", left_side[1], right_side[0]) - jnp.einsum("lij,lkj->lik", left_side[0], right_side[1])
    return real_part, imag_part


def pair_terms(sink_side, source, direct_ins, direct_coef, direct_entry, box_ins, box_coef, box_entry):
    sink_side = sink_side.astype(jnp.float32)
    source = source.astype(jnp.float32)
    loop_real = jnp.einsum("cgij,chij->gh", sink_side, source)
    loop_imag = jnp.einsum("gij,hij->gh", sink_side[1], source[0]) - jnp.einsum("gij,hij->gh", sink_side[0], source[1])
    real_left = loop_real[direct_ins[:, 0], direct_ins[:, 1]]
    imag_left = loop_imag[direct_ins[:, 0], direct_ins[:, 1]]
    real_right = loop_real[direct_ins[:, 2], direct_ins[:, 3]]
    imag_right = loop_imag[direct_ins[:, 2], direct_ins[:, 3]]
    direct_real = direct_coef * (real_left * real_right - imag_left * imag_right)
    direct_imag = direct_coef * (real_left * imag_right + imag_left * real_right)
    first_real, first_imag = adjoint_product(sink_side[:, box_ins[:, 0]], source[:, box_ins[:, 1]])
    second_real, second_imag = adjoint_product(source[:, box_ins[:, 3]], sink_side[:, box_ins[:, 2]])
    box_real = box_coef * jnp.sum(first_real * second_real + first_imag * second_imag, axis=(1, 2))
    box_imag = box_coef * jnp.sum(first_imag * second_real - first_real * second_imag, axis=(1, 2))
    direct_sum = jax.ops.segment_sum(jnp.stack([direct_real, direct_imag], 1), direct_entry, num_segments=ENTRIES)
    box_sum = jax.ops.segment_sum(jnp.stack([box_real, box_imag], 1), box_entry, num_segments=ENTRIES)
    return jnp.transpose(direct_sum - box_sum)


def reference(meson_fields, perambulators, direct_ins, direct_coef, direct_entry, box_ins, box_coef, box_entry):
    dressed = lax.map(lambda pieces: dress(pieces[0], pieces[1]), (jnp.moveaxis(meson_fields, 2, 0), jnp.moveaxis(perambulators, 1, 0)))
    outputs = []
    for distance in range(SEPARATIONS):
        def accumulate(totals, sink_time):
            source_time = ((sink_time + distance * SLICE_DEV) % SLICES).astype(jnp.int32)
            added = pair_terms(dressed[sink_time], dressed[source_time], direct_ins, direct_coef, direct_entry, box_ins, box_coef, box_entry)
            return totals + added, None
        totals, unused = lax.scan(accumulate, jnp.zeros((2, ENTRIES), jnp.float32), jnp.arange(SLICES, dtype=jnp.int32))
        outputs.append(totals / SLICES)
    return jnp.stack(outputs)
```

```python
import functools

import jax
import jax.numpy as jnp
from jax import lax
from jax.experimental import pallas as pl
from jax.experimental.pallas import tpu as pltpu
from jax.sharding import PartitionSpec as P

GROUP = 4
SEPARATIONS = 3
SLOTS = GROUP + SEPARATIONS - 1
MESH = pl.DeviceIdType.MESH
HIGHEST = lax.Precision.HIGHEST


def dress_kernel(fields, taus, out):
    count, rows = fields.shape[1], fields.shape[2]
    left = fields[0].reshape(count * rows, rows)
    right = fields[1].reshape(count * rows, rows)
    both = jnp.dot(left, taus[0], preferred_element_type=jnp.float32)
    both += jnp.dot(right, taus[1], preferred_element_type=jnp.float32)
    both = both.astype(jnp.bfloat16).reshape(count, GROUP, rows // GROUP, 2 * rows)
    for quarter in range(GROUP):
        for part in range(2):
            out[quarter, :, part] = both[:, quarter, :, part * rows : (part + 1) * rows]


def dress(fields, perambulators, block):
    _, inserts, modes, _ = fields.shape
    real_row = jnp.concatenate([perambulators[0], perambulators[1]], 1)
    imag_row = jnp.concatenate([-perambulators[1], perambulators[0]], 1)
    taus = jnp.stack([real_row, imag_row])
    return pl.pallas_call(
        dress_kernel,
        grid=(inserts // block,),
        in_specs=[
            pl.BlockSpec((2, block, modes, modes), lambda g: (0, g, 0, 0)),
            pl.BlockSpec((2, modes, 2 * modes), lambda g: (0, 0, 0)),
        ],
        out_specs=pl.BlockSpec((GROUP, block, 2, modes // GROUP, modes), lambda g: (0, g, 0, 0, 0)),
        out_shape=jax.ShapeDtypeStruct((GROUP, inserts, 2, modes // GROUP, modes), jnp.bfloat16),
        compiler_params=pltpu.CompilerParams(vmem_limit_bytes=40 * 2**20),
    )(fields, taus)


def missing_quarters(owner):
    far = 2 - 2 * (owner // 2)
    return (far, far + 1, owner + 1 - 2 * (owner % 2))


def pick_kernel(each, index, source, out):
    owner = pl.program_id(0) // each
    for place, quarter in enumerate(missing_quarters(owner)):
        out[0, 0, place] = source[quarter, 0]


def pick(quarters, index):
    total = index.shape[0]
    each = total // GROUP
    _, _, _, rows, modes = quarters.shape
    return pl.pallas_call(
        functools.partial(pick_kernel, each),
        grid_spec=pltpu.PrefetchScalarGridSpec(
            num_scalar_prefetch=1,
            grid=(total,),
            in_specs=[pl.BlockSpec((GROUP, 1, 2, rows, modes), lambda e, index: (0, index[e], 0, 0, 0))],
            out_specs=pl.BlockSpec(
                (1, 1, 3, 2, rows, modes), lambda e, index: (e // each, e % each, 0, 0, 0, 0)
            ),
        ),
        out_shape=jax.ShapeDtypeStruct((GROUP, each, 3, 2, rows, modes), jnp.bfloat16),
    )(index, quarters)


def other(rank, step):
    if step == 1:
        return rank + 1 - 2 * (rank % 2)
    if step == 2:
        return (rank + 2) % GROUP
    return GROUP - 1 - rank


def slot_of(rank, side):
    return rank + side * (GROUP - 1 - 2 * rank)


def exchange_kernel(n, lines, boxes, line_slots, box_slots, send_sem, recv_sem, local_sem):
    me = lax.axis_index("tm")
    rank = me % GROUP
    base = me - rank
    side = rank // 2
    half = boxes.shape[1] // 2
    target = (base + n - GROUP + 2 * side * GROUP) % n
    origin = (base + n + GROUP - 2 * side * GROUP) % n
    peers = [other(rank, step) for step in (2, 3, 1)]

    barrier = pltpu.get_barrier_semaphore()
    near = [base + peer for peer in peers]
    far = [group + 2 * side + core for group in (target, origin) for core in range(2)]
    for device in near + far:
        pl.semaphore_signal(barrier, inc=1, device_id={"tm": device}, device_id_type=MESH)
    pl.semaphore_wait(barrier, len(near) + len(far))

    def copies(order, owner, device, slot, whole):
        box_from, box_to = boxes.at[owner], box_slots.at[slot]
        if not whole:
            box_from, box_to = box_from.at[pl.ds(half, half)], box_to.at[pl.ds(half, half)]
        return [
            pltpu.make_async_remote_copy(
                src_ref=source,
                dst_ref=landing,
                send_sem=send_sem.at[order, kind],
                recv_sem=recv_sem.at[slot, kind],
                device_id={"tm": device},
                device_id_type=MESH,
            )
            for kind, (source, landing) in enumerate(
                ((lines.at[owner], line_slots.at[slot]), (box_from, box_to))
            )
        ]

    sent = []
    for order, peer in enumerate(peers):
        sent += copies(order, peer, base + peer, slot_of(rank, peer // 2), True)
        for copy in sent[-2:]:
            copy.start()
        if order < 2:
            owner = 2 * side + (rank + order) % 2
            sent += copies(3 + order, owner, target + owner, GROUP + slot_of(rank, side), False)
            for copy in sent[-2:]:
                copy.start()
    own = slot_of(rank, side)
    kept = [
        pltpu.make_async_copy(lines.at[rank], line_slots.at[own], local_sem.at[0]),
        pltpu.make_async_copy(boxes.at[rank], box_slots.at[own], local_sem.at[1]),
    ]
    for copy in kept:
        copy.start()
    for copy in kept:
        copy.wait()
    for copy in sent:
        copy.wait_send()
    for peer in peers:
        for copy in copies(0, rank, me, slot_of(peer, side), True):
            copy.wait_recv()
    for place in range(2):
        for copy in copies(0, rank, me, GROUP + place, False):
            copy.wait_recv()


def exchange(n, lines, boxes):
    return pl.pallas_call(
        functools.partial(exchange_kernel, n),
        in_specs=[pl.BlockSpec(memory_space=pl.ANY)] * 2,
        out_specs=[pl.BlockSpec(memory_space=pl.ANY)] * 2,
        out_shape=[
            jax.ShapeDtypeStruct((SLOTS, *lines.shape[1:]), jnp.bfloat16),
            jax.ShapeDtypeStruct((SLOTS, *boxes.shape[1:]), jnp.bfloat16),
        ],
        scratch_shapes=[
            pltpu.SemaphoreType.DMA((5, 2)),
            pltpu.SemaphoreType.DMA((SLOTS, 2)),
            pltpu.SemaphoreType.DMA((2,)),
        ],
        compiler_params=pltpu.CompilerParams(
            collective_id=0, has_side_effects=True, vmem_limit_bytes=2**20
        ),
    )(lines, boxes)


def pairs_kernel(terms, index, where, line, box, gram, traces, flat, plain, turned):
    slot = pl.program_id(0)
    inserts, _, rows, modes = line.shape[1:]
    owner = where[0]
    side = owner // 2
    each = 4 * terms

    @pl.when(slot == 0)
    def _():
        traces[...] = jnp.zeros_like(traces)

    step = 16
    for start in range(0, rows, step):
        block = line[0, :, :, start : start + step, :].reshape(2 * inserts, step, modes)
        flat[slot, :, start * modes : (start + step) * modes] = block.reshape(2 * inserts, step * modes)

    quarters = missing_quarters(owner)
    for entry in range(each):
        role, rest = divmod(entry, 2 * terms)
        term, which = divmod(rest, 2)
        spot = (role * terms + term) * 2 + which
        is_left = role == which

        def fill(quarter, values):
            at = pl.ds(pl.multiple_of(quarter * rows, rows), rows)
            real, imag = values
            plain[slot, spot, at, :modes] = real
            plain[slot, spot, at, modes:] = imag
            if is_left:
                spun = role * terms + term
                turned[slot, spun, at, :modes] = imag
                turned[slot, spun, at, modes:] = -real

        for place, quarter in enumerate(quarters):
            fill(quarter, (box[0, entry, place, 0], box[0, entry, place, 1]))
        ins = index[owner * each + entry]
        fill(owner, (line[0, ins, 0], line[0, ins, 1]))

    contract = (((1,), (1,)), ((), ()))
    for k in range(SEPARATIONS):
        sink = slot - k

        @pl.when((sink >= 0) & (sink < GROUP))
        def _(k=k, sink=sink):
            gram[sink, k] = lax.dot_general(
                flat[sink], flat[slot], contract, preferred_element_type=jnp.float32
            )
            for term in range(terms):
                a, a_turned = plain[sink, 2 * term], turned[sink, term]
                c = plain[sink, 2 * term + 1]
                b = plain[slot, 2 * terms + 2 * term]
                e, e_turned = plain[slot, 2 * terms + 2 * term + 1], turned[slot, terms + term]
                first_real = lax.dot_general(a, b, contract, preferred_element_type=jnp.float32)
                first_imag = lax.dot_general(a_turned, b, contract, preferred_element_type=jnp.float32)
                second_real = lax.dot_general(e, c, contract, preferred_element_type=jnp.float32)
                second_imag = lax.dot_general(e_turned, c, contract, preferred_element_type=jnp.float32)
                real = first_real * second_real + first_imag * second_imag
                imag = first_imag * second_real - first_real * second_imag
                for part, value in enumerate((real, imag)):
                    traces[k, term, part] += jnp.sum(value.reshape(-1, 8, modes), axis=0)


def pairs(index, rank, line_slots, box_slots):
    _, inserts, _, rows, modes = line_slots.shape
    each = box_slots.shape[1]
    terms = each // 4
    return pl.pallas_call(
        functools.partial(pairs_kernel, terms),
        grid_spec=pltpu.PrefetchScalarGridSpec(
            num_scalar_prefetch=2,
            grid=(SLOTS,),
            in_specs=[
                pl.BlockSpec((1, inserts, 2, rows, modes), lambda s, *_: (s, 0, 0, 0, 0)),
                pl.BlockSpec((1, each, 3, 2, rows, modes), lambda s, *_: (s, 0, 0, 0, 0, 0)),
            ],
            out_specs=[
                pl.BlockSpec((GROUP, SEPARATIONS, 2 * inserts, 2 * inserts), lambda s, *_: (0, 0, 0, 0)),
                pl.BlockSpec((SEPARATIONS, terms, 2, 8, modes), lambda s, *_: (0, 0, 0, 0, 0)),
            ],
            scratch_shapes=[
                pltpu.VMEM((SLOTS, 2 * inserts, rows * modes), jnp.bfloat16),
                pltpu.VMEM((SLOTS, each, modes, 2 * modes), jnp.bfloat16),
                pltpu.VMEM((SLOTS, 2 * terms, modes, 2 * modes), jnp.bfloat16),
            ],
        ),
        out_shape=[
            jax.ShapeDtypeStruct((GROUP, SEPARATIONS, 2 * inserts, 2 * inserts), jnp.float32),
            jax.ShapeDtypeStruct((SEPARATIONS, terms, 2, 8, modes), jnp.float32),
        ],
        compiler_params=pltpu.CompilerParams(vmem_limit_bytes=56 * 2**20),
    )(index, rank[None], line_slots, box_slots)


def local(
    entries,
    meson_fields,
    perambulators,
    direct_ins,
    direct_coef,
    direct_entry,
    box_ins,
    box_coef,
    box_entry,
):
    n = lax.axis_size("tm")
    me = lax.axis_index("tm")
    rank = me % GROUP
    base = me - rank
    right = rank >= 2
    inserts = meson_fields.shape[1]
    terms = box_ins.shape[0] // GROUP

    by_owner = box_ins.reshape(GROUP, terms, 4)
    by_owner = jnp.concatenate([by_owner[:2], by_owner[2:, :, ::-1]], 0)
    index = jnp.transpose(by_owner.reshape(GROUP, terms, 2, 2), (0, 3, 1, 2)).reshape(-1)

    lines = dress(meson_fields[:, :, 0], perambulators[:, 0], 4)
    boxes = pick(lines, index)
    line_slots, box_slots = exchange(n, lines, boxes)
    gram, traces = pairs(index, rank, line_slots, box_slots)

    gram = gram.reshape(GROUP, SEPARATIONS, inserts, 2, inserts, 2)
    loop_real = gram[:, :, :, 0, :, 0] + gram[:, :, :, 1, :, 1]
    loop_imag = gram[:, :, :, 1, :, 0] - gram[:, :, :, 0, :, 1]
    parts = jnp.stack([loop_real, loop_imag], 2)
    flipped = jnp.stack([jnp.swapaxes(loop_real, 2, 3), -jnp.swapaxes(loop_imag, 2, 3)], 2)
    parts = jnp.where(right, flipped, parts)
    slot = jnp.arange(GROUP, dtype=jnp.int32)[:, None]
    apart = jnp.arange(SEPARATIONS, dtype=jnp.int32)[None]
    sink_time = jnp.where(right, base + GROUP - 1 - slot - apart, base + slot) % n
    hot = (sink_time[..., None] == jnp.arange(n, dtype=jnp.int32)).astype(jnp.float32)
    spread = jnp.sum(hot[..., None, None, None] * parts[:, :, None], axis=0)
    spread = jnp.transpose(spread, (1, 0, 2, 3, 4))
    loops = lax.psum_scatter(spread, "tm", scatter_dimension=0, tiled=True)[0]

    inserted = jnp.arange(inserts, dtype=jnp.int32)[:, None]
    hots = [(direct_ins[:, p][None] == inserted).astype(jnp.float32) for p in range(4)]

    def lookup(row_hot, column_hot):
        picked = jnp.einsum("kcab,al->kcbl", loops, row_hot, precision=HIGHEST)
        return jnp.sum(picked * column_hot, axis=2)

    left, second = lookup(hots[0], hots[1]), lookup(hots[2], hots[3])
    direct_real = left[:, 0] * second[:, 0] - left[:, 1] * second[:, 1]
    direct_imag = left[:, 0] * second[:, 1] + left[:, 1] * second[:, 0]
    direct = direct_coef * jnp.stack([direct_real, direct_imag], 1)
    entry_hot = (direct_entry[:, None] == jnp.arange(entries, dtype=jnp.int32)).astype(jnp.float32)
    direct_sum = jnp.einsum("kcl,le->kce", direct, entry_hot, precision=HIGHEST)

    traces = jnp.sum(traces, axis=(3, 4))
    sign = jnp.stack([jnp.float32(1), jnp.where(right, -1.0, 1.0).astype(jnp.float32)])
    coef = lax.dynamic_slice(box_coef, (rank * terms,), (terms,))
    entry = lax.dynamic_slice(box_entry, (rank * terms,), (terms,))
    box_hot = (entry[:, None] == jnp.arange(entries, dtype=jnp.int32)).astype(jnp.float32)
    weighted = traces * coef[None, :, None] * sign
    box_sum = jnp.sum(weighted[..., None] * box_hot[None, :, None], axis=1)

    total = lax.psum_scatter(direct_sum - box_sum, "tm", scatter_dimension=2, tiled=True)
    return total / n


ENTRY_DEV = 4


def solution(mesh):
    placed = (
        P(None, None, ("cfg", "tm"), None, None),
        P(None, ("cfg", "tm"), None, None),
        P(),
        P(),
        P(),
        P(),
        P(),
        P(),
    )
    entries = ENTRY_DEV * mesh.shape["tm"]
    return jax.shard_map(
        functools.partial(local, entries),
        mesh=mesh,
        in_specs=placed,
        out_specs=P(None, None, ("cfg", "tm")),
        check_vma=False,
    )
```

```python
import functools

import jax
import jax.numpy as jnp
from jax import lax
from jax.experimental import pallas as pl
from jax.experimental.pallas import tpu as pltpu
from jax.sharding import PartitionSpec as P

GROUP = 4
SEPARATIONS = 3
SLOTS = GROUP + SEPARATIONS - 1
MESH = pl.DeviceIdType.MESH
HIGHEST = lax.Precision.HIGHEST


def dress_kernel(fields, taus, out):
    count, rows = fields.shape[1], fields.shape[2]
    left = fields[0].reshape(count * rows, rows)
    right = fields[1].reshape(count * rows, rows)
    both = jnp.dot(left, taus[0], preferred_element_type=jnp.float32)
    both += jnp.dot(right, taus[1], preferred_element_type=jnp.float32)
    both = both.astype(jnp.bfloat16).reshape(count, GROUP, rows // GROUP, 2 * rows)
    for quarter in range(GROUP):
        for part in range(2):
            out[quarter, :, part] = both[:, quarter, :, part * rows : (part + 1) * rows]


def dress(fields, perambulators, block):
    _, inserts, modes, _ = fields.shape
    real_row = jnp.concatenate([perambulators[0], perambulators[1]], 1)
    imag_row = jnp.concatenate([-perambulators[1], perambulators[0]], 1)
    taus = jnp.stack([real_row, imag_row])
    return pl.pallas_call(
        dress_kernel,
        grid=(inserts // block,),
        in_specs=[
            pl.BlockSpec((2, block, modes, modes), lambda g: (0, g, 0, 0)),
            pl.BlockSpec((2, modes, 2 * modes), lambda g: (0, 0, 0)),
        ],
        out_specs=pl.BlockSpec((GROUP, block, 2, modes // GROUP, modes), lambda g: (0, g, 0, 0, 0)),
        out_shape=jax.ShapeDtypeStruct((GROUP, inserts, 2, modes // GROUP, modes), jnp.bfloat16),
        compiler_params=pltpu.CompilerParams(vmem_limit_bytes=40 * 2**20),
    )(fields, taus)


def missing_quarters(owner):
    far = 2 - 2 * (owner // 2)
    return (far, far + 1, owner + 1 - 2 * (owner % 2))


def other(rank, step):
    if step == 1:
        return rank + 1 - 2 * (rank % 2)
    if step == 2:
        return (rank + 2) % GROUP
    return GROUP - 1 - rank


def slot_of(rank, side):
    return rank + side * (GROUP - 1 - 2 * rank)


def exchange_kernel(
    n, lines, index, line_slots, box_slots, boxes, send_sem, recv_sem, local_sem
):
    me = lax.axis_index("tm")
    rank = me % GROUP
    base = me - rank
    side = rank // 2
    half = boxes.shape[1] // 2
    target = (base + n - GROUP + 2 * side * GROUP) % n
    origin = (base + n + GROUP - 2 * side * GROUP) % n
    peers = [other(rank, step) for step in (2, 3, 1)]

    barrier = pltpu.get_barrier_semaphore()
    near = [base + peer for peer in peers]
    far = [group + 2 * side + core for group in (target, origin) for core in range(2)]
    for device in near + far:
        pl.semaphore_signal(barrier, inc=1, device_id={"tm": device}, device_id_type=MESH)
    pl.semaphore_wait(barrier, len(near) + len(far))

    def choose(owner):
        def body(entry, carry):
            for place, quarter in enumerate(missing_quarters(owner)):
                boxes[owner, entry, place] = lines[quarter, index[owner * 2 * half + entry]]
            return carry

        lax.fori_loop(0, 2 * half, body, 0)

    def copies(order, owner, device, slot, whole):
        box_from, box_to = boxes.at[owner], box_slots.at[slot]
        if not whole:
            box_from, box_to = box_from.at[pl.ds(half, half)], box_to.at[pl.ds(half, half)]
        return [
            pltpu.make_async_remote_copy(
                src_ref=source,
                dst_ref=landing,
                send_sem=send_sem.at[order, kind],
                recv_sem=recv_sem.at[slot, kind],
                device_id={"tm": device},
                device_id_type=MESH,
            )
            for kind, (source, landing) in enumerate(
                ((lines.at[owner], line_slots.at[slot]), (box_from, box_to))
            )
        ]

    sent = []
    for order, peer in enumerate(peers):
        sent.append(copies(order, peer, base + peer, slot_of(rank, peer // 2), True))
        if order < 2:
            owner = 2 * side + (rank + order) % 2
            sent.append(copies(3 + order, owner, target + owner, GROUP + slot_of(rank, side), False))
    for line_copy, _ in sent:
        line_copy.start()
    for owner in range(GROUP):
        choose(owner)
    for _, box_copy in sent:
        box_copy.start()
    own = slot_of(rank, side)
    kept = [
        pltpu.make_async_copy(lines.at[rank], line_slots.at[own], local_sem.at[0]),
        pltpu.make_async_copy(boxes.at[rank], box_slots.at[own], local_sem.at[1]),
    ]
    for copy in kept:
        copy.start()
    for copy in kept:
        copy.wait()
    for pair in sent:
        for copy in pair:
            copy.wait_send()
    for peer in peers:
        for copy in copies(0, rank, me, slot_of(peer, side), True):
            copy.wait_recv()
    for place in range(2):
        for copy in copies(0, rank, me, GROUP + place, False):
            copy.wait_recv()


def exchange(n, lines, index):
    _, inserts, _, rows, modes = lines.shape
    each = index.shape[0] // GROUP
    return pl.pallas_call(
        functools.partial(exchange_kernel, n),
        in_specs=[
            pl.BlockSpec(memory_space=pltpu.VMEM),
            pl.BlockSpec(memory_space=pltpu.SMEM),
        ],
        out_specs=[pl.BlockSpec(memory_space=pl.ANY)] * 2,
        out_shape=[
            jax.ShapeDtypeStruct((SLOTS, inserts, 2, rows, modes), jnp.bfloat16),
            jax.ShapeDtypeStruct((SLOTS, each, 3, 2, rows, modes), jnp.bfloat16),
        ],
        scratch_shapes=[
            pltpu.VMEM((GROUP, each, 3, 2, rows, modes), jnp.bfloat16),
            pltpu.SemaphoreType.DMA((5, 2)),
            pltpu.SemaphoreType.DMA((SLOTS, 2)),
            pltpu.SemaphoreType.DMA((2,)),
        ],
        compiler_params=pltpu.CompilerParams(
            collective_id=0, has_side_effects=True, vmem_limit_bytes=20 * 2**20
        ),
    )(lines, index)


def gather_loops_kernel(n, parts, total, landed, send_sem, recv_sem):
    me = lax.axis_index("tm")
    rank = me % GROUP
    base = me - rank
    side = rank // 2
    peers = [other(rank, step) for step in (2, 3, 1)]
    before = (base + n - GROUP) % n
    behind = (base + GROUP) % n

    barrier = pltpu.get_barrier_semaphore()
    near = [base + peer for peer in peers]
    far = [group + 2 * side + core for group in (before, behind) for core in range(2)]
    for device in near + far:
        pl.semaphore_signal(barrier, inc=1, device_id={"tm": device}, device_id_type=MESH)
    pl.semaphore_wait(barrier, len(near) + len(far))

    def copy_to(order, block, device, slot):
        return pltpu.make_async_remote_copy(
            src_ref=parts.at[block],
            dst_ref=landed.at[slot],
            send_sem=send_sem.at[order],
            recv_sem=recv_sem.at[slot],
            device_id={"tm": device},
            device_id_type=MESH,
        )

    sent = [copy_to(3 + core, core, before + 2 * side + core, GROUP + rank % 2) for core in range(2)]
    sent += [copy_to(order, 2 + peer, base + peer, rank) for order, peer in enumerate(peers)]
    for copy in sent:
        copy.start()
    for slot in peers + [GROUP, GROUP + 1]:
        copy_to(0, 0, me, slot).wait_recv()
    value = parts[2 + rank]
    for slot in peers + [GROUP, GROUP + 1]:
        value += landed[slot]
    total[...] = value
    for copy in sent:
        copy.wait_send()


def gather_loops(n, parts):
    return pl.pallas_call(
        functools.partial(gather_loops_kernel, n),
        in_specs=[pl.BlockSpec(memory_space=pltpu.VMEM)],
        out_specs=pl.BlockSpec(memory_space=pltpu.VMEM),
        out_shape=jax.ShapeDtypeStruct(parts.shape[1:], jnp.float32),
        scratch_shapes=[
            pltpu.VMEM((SLOTS, *parts.shape[1:]), jnp.float32),
            pltpu.SemaphoreType.DMA((5,)),
            pltpu.SemaphoreType.DMA((SLOTS,)),
        ],
        compiler_params=pltpu.CompilerParams(collective_id=1, has_side_effects=True),
    )(parts)


def sum_all_kernel(n, part, total, landed, send_sem, recv_sem):
    me = lax.axis_index("tm")
    barrier = pltpu.get_barrier_semaphore()

    def greet(step, carry):
        pl.semaphore_signal(barrier, inc=1, device_id={"tm": (me + step) % n}, device_id_type=MESH)
        return carry

    lax.fori_loop(1, n, greet, 0)
    pl.semaphore_wait(barrier, n - 1)

    def copy_to(step, slot):
        return pltpu.make_async_remote_copy(
            src_ref=part,
            dst_ref=landed.at[slot],
            send_sem=send_sem.at[step],
            recv_sem=recv_sem.at[slot],
            device_id={"tm": (me + step) % n},
            device_id_type=MESH,
        )

    def send(step, carry):
        copy_to(step, me).start()
        return carry

    lax.fori_loop(1, n, send, 0)

    def receive(step, value):
        slot = (me + step) % n
        copy_to(step, slot).wait_recv()
        return value + landed[slot]

    total[...] = lax.fori_loop(1, n, receive, part[...])

    def finish(step, carry):
        copy_to(step, me).wait_send()
        return carry

    lax.fori_loop(1, n, finish, 0)


def sum_all(n, part):
    return pl.pallas_call(
        functools.partial(sum_all_kernel, n),
        in_specs=[pl.BlockSpec(memory_space=pltpu.VMEM)],
        out_specs=pl.BlockSpec(memory_space=pltpu.VMEM),
        out_shape=jax.ShapeDtypeStruct(part.shape, jnp.float32),
        scratch_shapes=[
            pltpu.VMEM((n, *part.shape), jnp.float32),
            pltpu.SemaphoreType.DMA((n,)),
            pltpu.SemaphoreType.DMA((n,)),
        ],
        compiler_params=pltpu.CompilerParams(collective_id=2, has_side_effects=True),
    )(part)


def pairs_kernel(terms, index, where, line, box, gram, traces, flat, plain, turned):
    slot = pl.program_id(0)
    inserts, _, rows, modes = line.shape[1:]
    owner = where[0]
    side = owner // 2
    each = 4 * terms

    @pl.when(slot == 0)
    def _():
        traces[...] = jnp.zeros_like(traces)

    step = 16
    for start in range(0, rows, step):
        block = line[0, :, :, start : start + step, :].reshape(2 * inserts, step, modes)
        flat[slot, :, start * modes : (start + step) * modes] = block.reshape(2 * inserts, step * modes)

    quarters = missing_quarters(owner)
    for entry in range(each):
        role, rest = divmod(entry, 2 * terms)
        term, which = divmod(rest, 2)
        spot = (role * terms + term) * 2 + which
        is_left = role == which

        def fill(quarter, values):
            at = pl.ds(pl.multiple_of(quarter * rows, rows), rows)
            real, imag = values
            plain[slot, spot, at, :modes] = real
            plain[slot, spot, at, modes:] = imag
            if is_left:
                spun = role * terms + term
                turned[slot, spun, at, :modes] = imag
                turned[slot, spun, at, modes:] = -real

        for place, quarter in enumerate(quarters):
            fill(quarter, (box[0, entry, place, 0], box[0, entry, place, 1]))
        ins = index[owner * each + entry]
        fill(owner, (line[0, ins, 0], line[0, ins, 1]))

    contract = (((1,), (1,)), ((), ()))
    for k in range(SEPARATIONS):
        sink = slot - k

        @pl.when((sink >= 0) & (sink < GROUP))
        def _(k=k, sink=sink):
            gram[sink, k] = lax.dot_general(
                flat[sink], flat[slot], contract, preferred_element_type=jnp.float32
            )
            for term in range(terms):
                a, a_turned = plain[sink, 2 * term], turned[sink, term]
                c = plain[sink, 2 * term + 1]
                b = plain[slot, 2 * terms + 2 * term]
                e, e_turned = plain[slot, 2 * terms + 2 * term + 1], turned[slot, terms + term]
                first_real = lax.dot_general(a, b, contract, preferred_element_type=jnp.float32)
                first_imag = lax.dot_general(a_turned, b, contract, preferred_element_type=jnp.float32)
                second_real = lax.dot_general(e, c, contract, preferred_element_type=jnp.float32)
                second_imag = lax.dot_general(e_turned, c, contract, preferred_element_type=jnp.float32)
                real = first_real * second_real + first_imag * second_imag
                imag = first_imag * second_real - first_real * second_imag
                for part, value in enumerate((real, imag)):
                    traces[k, term, part] += jnp.sum(value.reshape(-1, 8, modes), axis=0)


def pairs(index, rank, line_slots, box_slots):
    _, inserts, _, rows, modes = line_slots.shape
    each = box_slots.shape[1]
    terms = each // 4
    return pl.pallas_call(
        functools.partial(pairs_kernel, terms),
        grid_spec=pltpu.PrefetchScalarGridSpec(
            num_scalar_prefetch=2,
            grid=(SLOTS,),
            in_specs=[
                pl.BlockSpec((1, inserts, 2, rows, modes), lambda s, *_: (s, 0, 0, 0, 0)),
                pl.BlockSpec((1, each, 3, 2, rows, modes), lambda s, *_: (s, 0, 0, 0, 0, 0)),
            ],
            out_specs=[
                pl.BlockSpec((GROUP, SEPARATIONS, 2 * inserts, 2 * inserts), lambda s, *_: (0, 0, 0, 0)),
                pl.BlockSpec((SEPARATIONS, terms, 2, 8, modes), lambda s, *_: (0, 0, 0, 0, 0)),
            ],
            scratch_shapes=[
                pltpu.VMEM((SLOTS, 2 * inserts, rows * modes), jnp.bfloat16),
                pltpu.VMEM((SLOTS, each, modes, 2 * modes), jnp.bfloat16),
                pltpu.VMEM((SLOTS, 2 * terms, modes, 2 * modes), jnp.bfloat16),
            ],
        ),
        out_shape=[
            jax.ShapeDtypeStruct((GROUP, SEPARATIONS, 2 * inserts, 2 * inserts), jnp.float32),
            jax.ShapeDtypeStruct((SEPARATIONS, terms, 2, 8, modes), jnp.float32),
        ],
        compiler_params=pltpu.CompilerParams(vmem_limit_bytes=56 * 2**20),
    )(index, rank[None], line_slots, box_slots)


def local(
    entries,
    meson_fields,
    perambulators,
    direct_ins,
    direct_coef,
    direct_entry,
    box_ins,
    box_coef,
    box_entry,
):
    n = lax.axis_size("tm")
    me = lax.axis_index("tm")
    rank = me % GROUP
    base = me - rank
    right = rank >= 2
    inserts = meson_fields.shape[1]
    terms = box_ins.shape[0] // GROUP

    by_owner = box_ins.reshape(GROUP, terms, 4)
    by_owner = jnp.concatenate([by_owner[:2], by_owner[2:, :, ::-1]], 0)
    index = jnp.transpose(by_owner.reshape(GROUP, terms, 2, 2), (0, 3, 1, 2)).reshape(-1)

    lines = dress(meson_fields[:, :, 0], perambulators[:, 0], 4)
    line_slots, box_slots = exchange(n, lines, index)
    gram, traces = pairs(index, rank, line_slots, box_slots)

    gram = gram.reshape(GROUP, SEPARATIONS, inserts, 2, inserts, 2)
    loop_real = gram[:, :, :, 0, :, 0] + gram[:, :, :, 1, :, 1]
    loop_imag = gram[:, :, :, 1, :, 0] - gram[:, :, :, 0, :, 1]
    parts = jnp.stack([loop_real, loop_imag], 2)
    flipped = jnp.stack([jnp.swapaxes(loop_real, 2, 3), -jnp.swapaxes(loop_imag, 2, 3)], 2)
    zero = jnp.zeros_like(parts[0, 0])
    from_left, from_right = [], []
    for v in range(SLOTS):
        for k in range(SEPARATIONS):
            slot = SLOTS - 1 - k - v
            from_left.append(parts[v - 2, k] if v >= 2 else zero)
            from_right.append(flipped[slot, k] if 0 <= slot < GROUP else zero)
    blocks = jnp.where(right, jnp.stack(from_right), jnp.stack(from_left))
    loops = gather_loops(n, blocks.reshape(SLOTS, -1, 128))
    loops = loops.reshape(SEPARATIONS, 2, inserts, inserts)

    inserted = jnp.arange(inserts, dtype=jnp.int32)[:, None]
    hots = [(direct_ins[:, p][None] == inserted).astype(jnp.float32) for p in range(4)]

    def lookup(row_hot, column_hot):
        picked = jnp.einsum("kcab,al->kcbl", loops, row_hot, precision=HIGHEST)
        return jnp.sum(picked * column_hot, axis=2)

    left, second = lookup(hots[0], hots[1]), lookup(hots[2], hots[3])
    direct_real = left[:, 0] * second[:, 0] - left[:, 1] * second[:, 1]
    direct_imag = left[:, 0] * second[:, 1] + left[:, 1] * second[:, 0]
    direct = direct_coef * jnp.stack([direct_real, direct_imag], 1)
    entry_hot = (direct_entry[:, None] == jnp.arange(entries, dtype=jnp.int32)).astype(jnp.float32)
    direct_sum = jnp.einsum("kcl,le->kce", direct, entry_hot, precision=HIGHEST)

    traces = jnp.sum(traces, axis=(3, 4))
    sign = jnp.stack([jnp.float32(1), jnp.where(right, -1.0, 1.0).astype(jnp.float32)])
    coef = lax.dynamic_slice(box_coef, (rank * terms,), (terms,))
    entry = lax.dynamic_slice(box_entry, (rank * terms,), (terms,))
    box_hot = (entry[:, None] == jnp.arange(entries, dtype=jnp.int32)).astype(jnp.float32)
    weighted = traces * coef[None, :, None] * sign
    box_sum = jnp.sum(weighted[..., None] * box_hot[None, :, None], axis=1)

    partial = (direct_sum - box_sum).reshape(2 * SEPARATIONS, entries)
    rows, lanes = -2 * SEPARATIONS % 8, -entries % 128
    total = sum_all(n, jnp.pad(partial, ((0, rows), (0, lanes))))
    share = entries // n
    mine = lax.dynamic_slice(total, (0, me * share), (2 * SEPARATIONS, share))
    return mine.reshape(SEPARATIONS, 2, share) / n


ENTRY_DEV = 4


def solution(mesh):
    placed = (
        P(None, None, ("cfg", "tm"), None, None),
        P(None, ("cfg", "tm"), None, None),
        P(),
        P(),
        P(),
        P(),
        P(),
        P(),
    )
    entries = ENTRY_DEV * mesh.shape["tm"]
    return jax.shard_map(
        functools.partial(local, entries),
        mesh=mesh,
        in_specs=placed,
        out_specs=P(None, None, ("cfg", "tm")),
        check_vma=False,
    )
```

```python
import functools

import jax
import jax.numpy as jnp
from jax import lax
from jax.experimental import pallas as pl
from jax.experimental.pallas import tpu as pltpu
from jax.sharding import PartitionSpec as P

GROUP = 4
SEPARATIONS = 3
SLOTS = GROUP + SEPARATIONS - 1
MESH = pl.DeviceIdType.MESH
HIGHEST = lax.Precision.HIGHEST


def dress_kernel(fields, taus, out):
    count, rows = fields.shape[1], fields.shape[2]
    left = fields[0].reshape(count * rows, rows)
    right = fields[1].reshape(count * rows, rows)
    both = jnp.dot(left, taus[0], preferred_element_type=jnp.float32)
    both += jnp.dot(right, taus[1], preferred_element_type=jnp.float32)
    both = both.astype(jnp.bfloat16).reshape(count, GROUP, rows // GROUP, 2 * rows)
    for quarter in range(GROUP):
        for part in range(2):
            out[quarter, part] = both[:, quarter, :, part * rows : (part + 1) * rows]


def dress(fields, perambulators, block):
    _, inserts, modes, _ = fields.shape
    real_row = jnp.concatenate([perambulators[0], perambulators[1]], 1)
    imag_row = jnp.concatenate([-perambulators[1], perambulators[0]], 1)
    taus = jnp.stack([real_row, imag_row])
    return pl.pallas_call(
        dress_kernel,
        grid=(inserts // block,),
        in_specs=[
            pl.BlockSpec((2, block, modes, modes), lambda g: (0, g, 0, 0)),
            pl.BlockSpec((2, modes, 2 * modes), lambda g: (0, 0, 0)),
        ],
        out_specs=pl.BlockSpec((GROUP, 2, block, modes // GROUP, modes), lambda g: (0, 0, g, 0, 0)),
        out_shape=jax.ShapeDtypeStruct((GROUP, 2, inserts, modes // GROUP, modes), jnp.bfloat16),
        compiler_params=pltpu.CompilerParams(vmem_limit_bytes=40 * 2**20),
    )(fields, taus)


def missing_quarters(owner):
    far = 2 - 2 * (owner // 2)
    return (far, far + 1, owner + 1 - 2 * (owner % 2))


def other(rank, step):
    if step == 1:
        return rank + 1 - 2 * (rank % 2)
    if step == 2:
        return (rank + 2) % GROUP
    return GROUP - 1 - rank


def slot_of(rank, side):
    return rank + side * (GROUP - 1 - 2 * rank)


def exchange_kernel(
    n, lines, index, line_slots, box_slots, held, boxes, send_sem, recv_sem, local_sem
):
    me = lax.axis_index("tm")
    rank = me % GROUP
    base = me - rank
    side = rank // 2
    half = boxes.shape[1] // 2
    target = (base + n - GROUP + 2 * side * GROUP) % n
    origin = (base + n + GROUP - 2 * side * GROUP) % n
    peers = [other(rank, step) for step in (2, 3, 1)]

    barrier = pltpu.get_barrier_semaphore()
    near = [base + peer for peer in peers]
    far = [group + 2 * side + core for group in (target, origin) for core in range(2)]
    for device in near + far:
        pl.semaphore_signal(barrier, inc=1, device_id={"tm": device}, device_id_type=MESH)
    pl.semaphore_wait(barrier, len(near) + len(far))

    def choose(owner):
        def body(entry, carry):
            ins = index[owner * 2 * half + entry]
            for place, quarter in enumerate(missing_quarters(owner)):
                for part in range(2):
                    boxes[owner, entry, place, part] = held[quarter, part, ins]
            return carry

        lax.fori_loop(0, 2 * half, body, 0)

    def copies(order, owner, device, slot, whole):
        box_from, box_to = boxes.at[owner], box_slots.at[slot]
        if not whole:
            box_from, box_to = box_from.at[pl.ds(half, half)], box_to.at[pl.ds(half, half)]
        return [
            pltpu.make_async_remote_copy(
                src_ref=source,
                dst_ref=landing,
                send_sem=send_sem.at[order, kind],
                recv_sem=recv_sem.at[slot, kind],
                device_id={"tm": device},
                device_id_type=MESH,
            )
            for kind, (source, landing) in enumerate(
                ((lines.at[owner], line_slots.at[slot]), (box_from, box_to))
            )
        ]

    sent = []
    for order, peer in enumerate(peers):
        sent.append(copies(order, peer, base + peer, slot_of(rank, peer // 2), True))
        if order < 2:
            owner = 2 * side + (rank + order) % 2
            sent.append(copies(3 + order, owner, target + owner, GROUP + slot_of(rank, side), False))
    keep = pltpu.make_async_copy(lines, held, local_sem.at[2])
    keep.start()
    for line_copy, _ in sent:
        line_copy.start()
    keep.wait()
    for owner in range(GROUP):
        choose(owner)
    for _, box_copy in sent:
        box_copy.start()
    own = slot_of(rank, side)
    kept = [
        pltpu.make_async_copy(lines.at[rank], line_slots.at[own], local_sem.at[0]),
        pltpu.make_async_copy(boxes.at[rank], box_slots.at[own], local_sem.at[1]),
    ]
    for copy in kept:
        copy.start()
    for copy in kept:
        copy.wait()
    for pair in sent:
        for copy in pair:
            copy.wait_send()
    for peer in peers:
        for copy in copies(0, rank, me, slot_of(peer, side), True):
            copy.wait_recv()
    for place in range(2):
        for copy in copies(0, rank, me, GROUP + place, False):
            copy.wait_recv()


def exchange(n, lines, index):
    _, _, inserts, rows, modes = lines.shape
    each = index.shape[0] // GROUP
    return pl.pallas_call(
        functools.partial(exchange_kernel, n),
        in_specs=[
            pl.BlockSpec(memory_space=pl.ANY),
            pl.BlockSpec(memory_space=pltpu.SMEM),
        ],
        out_specs=[pl.BlockSpec(memory_space=pl.ANY)] * 2,
        out_shape=[
            jax.ShapeDtypeStruct((SLOTS, 2, inserts, rows, modes), jnp.bfloat16),
            jax.ShapeDtypeStruct((SLOTS, each, 3, 2, rows, modes), jnp.bfloat16),
        ],
        scratch_shapes=[
            pltpu.VMEM(lines.shape, jnp.bfloat16),
            pltpu.VMEM((GROUP, each, 3, 2, rows, modes), jnp.bfloat16),
            pltpu.SemaphoreType.DMA((5, 2)),
            pltpu.SemaphoreType.DMA((SLOTS, 2)),
            pltpu.SemaphoreType.DMA((3,)),
        ],
        compiler_params=pltpu.CompilerParams(
            collective_id=0, has_side_effects=True, vmem_limit_bytes=20 * 2**20
        ),
    )(lines, index)


def gather_loops_kernel(n, parts, total, landed, send_sem, recv_sem):
    me = lax.axis_index("tm")
    rank = me % GROUP
    base = me - rank
    side = rank // 2
    peers = [other(rank, step) for step in (2, 3, 1)]
    before = (base + n - GROUP) % n
    behind = (base + GROUP) % n

    barrier = pltpu.get_barrier_semaphore()
    near = [base + peer for peer in peers]
    far = [group + 2 * side + core for group in (before, behind) for core in range(2)]
    for device in near + far:
        pl.semaphore_signal(barrier, inc=1, device_id={"tm": device}, device_id_type=MESH)
    pl.semaphore_wait(barrier, len(near) + len(far))

    def copy_to(order, block, device, slot):
        return pltpu.make_async_remote_copy(
            src_ref=parts.at[block],
            dst_ref=landed.at[slot],
            send_sem=send_sem.at[order],
            recv_sem=recv_sem.at[slot],
            device_id={"tm": device},
            device_id_type=MESH,
        )

    sent = [copy_to(3 + core, core, before + 2 * side + core, GROUP + rank % 2) for core in range(2)]
    sent += [copy_to(order, 2 + peer, base + peer, rank) for order, peer in enumerate(peers)]
    for copy in sent:
        copy.start()
    for slot in peers + [GROUP, GROUP + 1]:
        copy_to(0, 0, me, slot).wait_recv()
    value = parts[2 + rank]
    for slot in peers + [GROUP, GROUP + 1]:
        value += landed[slot]
    total[...] = value
    for copy in sent:
        copy.wait_send()


def gather_loops(n, parts):
    return pl.pallas_call(
        functools.partial(gather_loops_kernel, n),
        in_specs=[pl.BlockSpec(memory_space=pltpu.VMEM)],
        out_specs=pl.BlockSpec(memory_space=pltpu.VMEM),
        out_shape=jax.ShapeDtypeStruct(parts.shape[1:], jnp.float32),
        scratch_shapes=[
            pltpu.VMEM((SLOTS, *parts.shape[1:]), jnp.float32),
            pltpu.SemaphoreType.DMA((5,)),
            pltpu.SemaphoreType.DMA((SLOTS,)),
        ],
        compiler_params=pltpu.CompilerParams(collective_id=1, has_side_effects=True),
    )(parts)


def sum_all_kernel(n, part, total, landed, send_sem, recv_sem):
    me = lax.axis_index("tm")
    barrier = pltpu.get_barrier_semaphore()

    def greet(step, carry):
        pl.semaphore_signal(barrier, inc=1, device_id={"tm": (me + step) % n}, device_id_type=MESH)
        return carry

    lax.fori_loop(1, n, greet, 0)
    pl.semaphore_wait(barrier, n - 1)

    def copy_to(step, slot):
        return pltpu.make_async_remote_copy(
            src_ref=part,
            dst_ref=landed.at[slot],
            send_sem=send_sem.at[step],
            recv_sem=recv_sem.at[slot],
            device_id={"tm": (me + step) % n},
            device_id_type=MESH,
        )

    def send(step, carry):
        copy_to(step, me).start()
        return carry

    lax.fori_loop(1, n, send, 0)

    def receive(step, value):
        slot = (me + step) % n
        copy_to(step, slot).wait_recv()
        return value + landed[slot]

    total[...] = lax.fori_loop(1, n, receive, part[...])

    def finish(step, carry):
        copy_to(step, me).wait_send()
        return carry

    lax.fori_loop(1, n, finish, 0)


def sum_all(n, part):
    return pl.pallas_call(
        functools.partial(sum_all_kernel, n),
        in_specs=[pl.BlockSpec(memory_space=pltpu.VMEM)],
        out_specs=pl.BlockSpec(memory_space=pltpu.VMEM),
        out_shape=jax.ShapeDtypeStruct(part.shape, jnp.float32),
        scratch_shapes=[
            pltpu.VMEM((n, *part.shape), jnp.float32),
            pltpu.SemaphoreType.DMA((n,)),
            pltpu.SemaphoreType.DMA((n,)),
        ],
        compiler_params=pltpu.CompilerParams(collective_id=2, has_side_effects=True),
    )(part)


def pairs_kernel(terms, index, where, line, box, loops, traces, flat, plain, turned):
    slot = pl.program_id(0)
    _, inserts, rows, modes = line.shape[1:]
    owner = where[0]
    side = owner // 2
    each = 4 * terms

    @pl.when(slot == 0)
    def _():
        traces[...] = jnp.zeros_like(traces)
        loops[...] = jnp.zeros_like(loops)

    step = 16
    for start in range(0, rows, step):
        block = line[0, :, :, start : start + step, :].reshape(2 * inserts, step, modes)
        flat[slot, :, start * modes : (start + step) * modes] = block.reshape(2 * inserts, step * modes)

    quarters = missing_quarters(owner)
    for entry in range(each):
        role, rest = divmod(entry, 2 * terms)
        term, which = divmod(rest, 2)
        spot = (role * terms + term) * 2 + which
        is_left = role == which

        def fill(quarter, values):
            at = pl.ds(pl.multiple_of(quarter * rows, rows), rows)
            real, imag = values
            plain[slot, spot, at, :modes] = real
            plain[slot, spot, at, modes:] = imag
            if is_left:
                spun = role * terms + term
                turned[slot, spun, at, :modes] = imag
                turned[slot, spun, at, modes:] = -real

        for place, quarter in enumerate(quarters):
            fill(quarter, (box[0, entry, place, 0], box[0, entry, place, 1]))
        ins = index[owner * each + entry]
        fill(owner, (line[0, 0, ins], line[0, 1, ins]))

    contract = (((1,), (1,)), ((), ()))
    for k in range(SEPARATIONS):
        sink = slot - k

        @pl.when((sink >= 0) & (sink < GROUP))
        def _(k=k, sink=sink):
            gram = lax.dot_general(
                flat[sink + side * k],
                flat[slot - side * k],
                contract,
                preferred_element_type=jnp.float32,
            )
            block = jnp.where(side == 0, sink + 2, SLOTS - 1 - k - sink)
            loops[block, k, 0] = gram[:inserts, :inserts] + gram[inserts:, inserts:]
            loops[block, k, 1] = gram[inserts:, :inserts] - gram[:inserts, inserts:]
            for term in range(terms):
                a, a_turned = plain[sink, 2 * term], turned[sink, term]
                c = plain[sink, 2 * term + 1]
                b = plain[slot, 2 * terms + 2 * term]
                e, e_turned = plain[slot, 2 * terms + 2 * term + 1], turned[slot, terms + term]
                first_real = lax.dot_general(a, b, contract, preferred_element_type=jnp.float32)
                first_imag = lax.dot_general(a_turned, b, contract, preferred_element_type=jnp.float32)
                second_real = lax.dot_general(e, c, contract, preferred_element_type=jnp.float32)
                second_imag = lax.dot_general(e_turned, c, contract, preferred_element_type=jnp.float32)
                real = first_real * second_real + first_imag * second_imag
                imag = first_imag * second_real - first_real * second_imag
                for part, value in enumerate((real, imag)):
                    traces[k, term, part] += jnp.sum(value.reshape(-1, 8, modes), axis=0)


def pairs(index, rank, line_slots, box_slots):
    _, _, inserts, rows, modes = line_slots.shape
    each = box_slots.shape[1]
    terms = each // 4
    return pl.pallas_call(
        functools.partial(pairs_kernel, terms),
        grid_spec=pltpu.PrefetchScalarGridSpec(
            num_scalar_prefetch=2,
            grid=(SLOTS,),
            in_specs=[
                pl.BlockSpec((1, 2, inserts, rows, modes), lambda s, *_: (s, 0, 0, 0, 0)),
                pl.BlockSpec((1, each, 3, 2, rows, modes), lambda s, *_: (s, 0, 0, 0, 0, 0)),
            ],
            out_specs=[
                pl.BlockSpec((SLOTS, SEPARATIONS, 2, inserts, inserts), lambda s, *_: (0, 0, 0, 0, 0)),
                pl.BlockSpec((SEPARATIONS, terms, 2, 8, modes), lambda s, *_: (0, 0, 0, 0, 0)),
            ],
            scratch_shapes=[
                pltpu.VMEM((SLOTS, 2 * inserts, rows * modes), jnp.bfloat16),
                pltpu.VMEM((SLOTS, each, modes, 2 * modes), jnp.bfloat16),
                pltpu.VMEM((SLOTS, 2 * terms, modes, 2 * modes), jnp.bfloat16),
            ],
        ),
        out_shape=[
            jax.ShapeDtypeStruct((SLOTS, SEPARATIONS, 2, inserts, inserts), jnp.float32),
            jax.ShapeDtypeStruct((SEPARATIONS, terms, 2, 8, modes), jnp.float32),
        ],
        compiler_params=pltpu.CompilerParams(vmem_limit_bytes=56 * 2**20),
    )(index, rank[None], line_slots, box_slots)


def local(
    entries,
    meson_fields,
    perambulators,
    direct_ins,
    direct_coef,
    direct_entry,
    box_ins,
    box_coef,
    box_entry,
):
    n = lax.axis_size("tm")
    me = lax.axis_index("tm")
    rank = me % GROUP
    right = rank >= 2
    inserts = meson_fields.shape[1]
    terms = box_ins.shape[0] // GROUP

    by_owner = box_ins.reshape(GROUP, terms, 4)
    by_owner = jnp.concatenate([by_owner[:2], by_owner[2:, :, ::-1]], 0)
    index = jnp.transpose(by_owner.reshape(GROUP, terms, 2, 2), (0, 3, 1, 2)).reshape(-1)

    lines = dress(meson_fields[:, :, 0], perambulators[:, 0], 4)
    line_slots, box_slots = exchange(n, lines, index)
    blocks, traces = pairs(index, rank, line_slots, box_slots)
    loops = gather_loops(n, blocks)

    inserted = jnp.arange(inserts, dtype=jnp.int32)[:, None]
    hots = [(direct_ins[:, p][None] == inserted).astype(jnp.float32) for p in range(4)]

    def lookup(row_hot, column_hot):
        picked = jnp.einsum("kcab,al->kcbl", loops, row_hot, precision=HIGHEST)
        return jnp.sum(picked * column_hot, axis=2)

    left, second = lookup(hots[0], hots[1]), lookup(hots[2], hots[3])
    direct_real = left[:, 0] * second[:, 0] - left[:, 1] * second[:, 1]
    direct_imag = left[:, 0] * second[:, 1] + left[:, 1] * second[:, 0]
    direct = direct_coef * jnp.stack([direct_real, direct_imag], 1)
    entry_hot = (direct_entry[:, None] == jnp.arange(entries, dtype=jnp.int32)).astype(jnp.float32)
    direct_sum = jnp.einsum("kcl,le->kce", direct, entry_hot, precision=HIGHEST)

    traces = jnp.sum(traces, axis=(3, 4))
    sign = jnp.stack([jnp.float32(1), jnp.where(right, -1.0, 1.0).astype(jnp.float32)])
    coef = lax.dynamic_slice(box_coef, (rank * terms,), (terms,))
    entry = lax.dynamic_slice(box_entry, (rank * terms,), (terms,))
    box_hot = (entry[:, None] == jnp.arange(entries, dtype=jnp.int32)).astype(jnp.float32)
    weighted = traces * coef[None, :, None] * sign
    box_sum = jnp.sum(weighted[..., None] * box_hot[None, :, None], axis=1)

    partial = (direct_sum - box_sum).reshape(2 * SEPARATIONS, entries)
    rows, lanes = -2 * SEPARATIONS % 8, -entries % 128
    total = sum_all(n, jnp.pad(partial, ((0, rows), (0, lanes))))
    share = entries // n
    mine = lax.dynamic_slice(total, (0, me * share), (2 * SEPARATIONS, share))
    return mine.reshape(SEPARATIONS, 2, share) / n


ENTRY_DEV = 4


def solution(mesh):
    placed = (
        P(None, None, ("cfg", "tm"), None, None),
        P(None, ("cfg", "tm"), None, None),
        P(),
        P(),
        P(),
        P(),
        P(),
        P(),
    )
    entries = ENTRY_DEV * mesh.shape["tm"]
    return jax.shard_map(
        functools.partial(local, entries),
        mesh=mesh,
        in_specs=placed,
        out_specs=P(None, None, ("cfg", "tm")),
        check_vma=False,
    )
```
